256 devices in a mesh: ctx: 16 (over z_hi, y, core), chan: 16 (over z_lo, x).
Axes of the slice: x: 4, y: 4, z: 8 (z_hi: 2, z_lo: 4; z = z_hi * 4 + z_lo), core: 2. Of those that a mesh axis runs over, the one named last changes fastest.
Arguments:
- signal: bfloat16 [4096, 2048], P('chan', 'ctx'), may hold values from -6 to 6
- gating: bfloat16 [4096, 2048], P('chan', 'ctx'), may hold values from -6 to 6
- skip_gain: float32 [4096], P('chan'), may hold values from -4 to 4
- spectrum: float32 [2, 4096, 32, 128], P(None, 'chan', 'ctx'), may hold values from -6 to 6
- out_weight: bfloat16 [4096, 4096], P(None, 'chan'), may hold values from -0.125 to 0.125
- cotangent: bfloat16 [2048, 4096], P('ctx', 'chan'), may hold values from -1.5 to 1.5
Outputs:
- output: bfloat16 [2048, 4096], P('ctx', 'chan')
- grad_signal: bfloat16 [4096, 2048], P('chan', 'ctx')
- grad_gating: bfloat16 [4096, 2048], P('chan', 'ctx')
- grad_spectrum: float32 [2, 4096, 32, 128], P(None, 'chan', 'ctx')
The draws below stay inside these ranges and needn't reach their ends.
All inputs are finite; a program needn't handle non-finite values.
Results may differ from the reference program's by a relative error of at most 0.0054.
Values may be sent and summed in bfloat16 or wider, within the bound.
No kernel may reach another device: no remote copies, remote signals or barrier semaphores. Data moves between devices by JAX's collectives and lax.ppermute only.
A program may use at most 64 MiB of HBM per device.

```python
import jax
import jax.numpy as jnp
import numpy as np
from jax import lax

D = 4096
LD = 128
C = 4096
L = 2048
KB = 32
N_CTX = 16


def spiked(entries, rng, source, target, parts, factor):
    def block_of(dim):
        return (jnp.arange(entries.shape[dim]) // (entries.shape[dim] // parts)).reshape((-1,) + (1,) * (entries.ndim - 1 - dim))

    one_side = jax.random.permutation(rng, parts)[block_of(target)]
    second = (block_of(target) + parts // 2) % parts
    return jnp.where((block_of(source) == one_side) | (block_of(source) == second), factor * entries, entries)


def block_levels(key, shape, shards, low, largest):
    loudness, own = 1.0, jax.random.fold_in(key, 6)
    for dim, shards_of in shards:
        steps = jnp.exp(jax.random.uniform(jax.random.fold_in(own, dim), (shards_of,), jnp.float32, low / len(shards), largest / len(shards)))
        loudness = loudness * jnp.repeat(steps, shape[dim] // shards_of).reshape([-1 if axis == dim else 1 for axis in range(len(shape))])
    return loudness


def noise(own_key, extent, width, reach, cuts=(), kind=jnp.bfloat16):
    values = jax.random.normal(own_key, extent, jnp.float32) * width
    if len(cuts) > 0:
        values = block_levels(own_key, extent, cuts, -0.22, 0.18) * values
    return jnp.clip(values, min=-reach, max=reach).astype(kind)


def noise_with(stream_key, shape, width, bound, cuts, heavy, kind=jnp.bfloat16):
    result = width * jax.random.normal(stream_key, shape, jnp.float32)
    if cuts:
        result = result * block_levels(stream_key, shape, cuts, -0.22, 0.18)
    return jnp.clip(spiked(result, jax.random.fold_in(stream_key, 3), *heavy), -bound, bound).astype(kind)


def setup_inputs(seed: int = 0) -> dict:
    streams_of = jax.random.split(jax.random.key(seed), 7)
    signal = noise(streams_of[0], (C, L), 1.0, 6.0, ((0, 16), (1, 16)))
    gating = noise(streams_of[1], (C, L), 1.0, 6.0, ((0, 16), (1, 16)))
    skip_gain = noise(streams_of[2], (C,), 1.0, 4.0, ((0, 16),), jnp.float32)
    spectrum = noise(streams_of[3], (2, C, KB, LD), 1.0, 6.0, ((1, 16), (2, 16)), jnp.float32)
    out_weight = noise_with(streams_of[4], (C, D), C ** -0.5, 0.125, ((1, 16),), (1, 0, 16, 2.0))
    cotangent = noise(streams_of[5], (L, D), 0.25, 1.5, ((0, 16), (1, 16)))
    return {"signal": signal, "gating": gating, "skip_gain": skip_gain, "spectrum": spectrum, "out_weight": out_weight, "cotangent": cotangent}


def reverse_bits(entry_count):
    bit_count = entry_count.bit_length() - 1
    table_out = []
    for entry_id in range(entry_count):
        reversed_id = 0
        for bit_place in range(bit_count):
            reversed_id = reversed_id * 2 + (entry_id >> bit_place) % 2
        table_out.append(reversed_id)
    return np.array(table_out, dtype=np.int32)


def residue_perm():
    bit_order = reverse_bits(N_CTX)
    kb_index = np.arange(KB)
    return 2 * bit_order[kb_index // 2] + kb_index % 2


def reference(signal, gating, skip_gain, spectrum, out_weight, cotangent):
    full_length = 2 * L
    class_perm = residue_perm()
    arranged = spectrum[:, :, class_perm, :]
    arranged = jnp.transpose(arranged, (0, 1, 3, 2)).reshape(2, C, LD * KB)
    filter_full = lax.complex(arranged[0], arranged[1])
    signal_f32 = signal.astype(jnp.float32)
    gate_f32 = gating.astype(jnp.float32)
    padded = jnp.pad(signal_f32, ((0, 0), (0, L)))
    signal_freq = jnp.fft.fft(padded, axis=1)
    conv_out = jnp.real(jnp.fft.ifft(filter_full * signal_freq, axis=1))[:, :L]
    pre_gate = conv_out + skip_gain[:, None] * signal_f32
    mixed_out = (gate_f32 * pre_gate).astype(jnp.bfloat16)
    output = jnp.dot(mixed_out.T, out_weight, preferred_element_type=jnp.float32).astype(jnp.bfloat16)
    grad_mixed = jnp.dot(out_weight, cotangent.T, preferred_element_type=jnp.float32)
    grad_pre = (gate_f32 * grad_mixed).astype(jnp.bfloat16)
    pre_f32 = lax.optimization_barrier(grad_pre).astype(jnp.float32)
    grad_freq = jnp.fft.fft(jnp.pad(pre_f32, ((0, 0), (0, L))), axis=1)
    back_out = jnp.real(jnp.fft.ifft(jnp.conj(filter_full) * grad_freq, axis=1))[:, :L]
    grad_signal = (back_out + skip_gain[:, None] * pre_f32).astype(jnp.bfloat16)
    grad_gating = (grad_mixed * pre_gate).astype(jnp.bfloat16)
    cross_term = jnp.conj(grad_freq) * signal_freq / full_length
    stacked = jnp.stack([jnp.real(cross_term), -jnp.imag(cross_term)])
    stacked = jnp.transpose(stacked.reshape(2, C, LD, KB), (0, 1, 3, 2))
    grad_spectrum = stacked[:, :, class_perm, :].astype(jnp.float32)
    return output, grad_signal, grad_gating, grad_spectrum
```

```python
import math

import jax
import jax.numpy as jnp
import numpy as np
from jax import lax
from jax.experimental import pallas as pl
from jax.experimental.pallas import tpu as pltpu
from jax.sharding import PartitionSpec as P

F32 = jnp.float32
BF16 = jnp.bfloat16
HIGHEST = lax.Precision.HIGHEST
VMEM = pl.BlockSpec(memory_space=pltpu.VMEM)
SMEM = pl.BlockSpec(memory_space=pltpu.SMEM)

N_CTX = 16
N_CHAN = 16
SPAN = 128
FULL = 2 * N_CTX * SPAN


def swap(block, axis, mask):
    return lax.ppermute(block, axis, [(i, i ^ mask) for i in range(16)])


def rev4(number):
    return int(f"{number:04b}"[::-1], 2)


def phase(turns, modulus):
    angle = (turns % modulus) * (2.0 * math.pi / modulus)
    return np.cos(angle), np.sin(angle)


def tables():
    ranks = np.arange(N_CTX)
    residues = np.array([[2 * rev4(r) + e for e in range(2)] for r in ranks])
    slots = ranks[:, None] ^ ranks[None, :]
    turn = np.stack(phase(slots[:, None, :] * residues[:, :, None], 32), 1)
    twid = np.stack(phase(residues[:, :, None] * np.arange(SPAN), FULL), 1)
    cos, sin = phase(np.arange(SPAN)[:, None] * np.arange(SPAN), SPAN)
    inner = np.block([[cos, -sin], [sin, cos]])
    return (
        turn.reshape(N_CTX, 64).astype(np.float32),
        twid.reshape(N_CTX, 4, SPAN).astype(np.float32),
        inner.astype(np.float32),
    )


def cost(flops, moved):
    return pl.CostEstimate(flops=flops, bytes_accessed=moved, transcendentals=0)


CHUNK = 32


def spread(slot_refs, turn_ref, twid_ref, held_ref):
    rows = held_ref.shape[1]

    def step(n, _):
        at = pl.ds(pl.multiple_of(n * CHUNK, CHUNK), CHUNK)
        acc = [jnp.zeros((CHUNK, SPAN), F32) for _ in range(4)]
        for i, (ref, place) in enumerate(slot_refs):
            x = (ref[at, :] if place is None else ref[place, at, :]).astype(F32)
            for e in range(2):
                acc[2 * e] += x * turn_ref[e * 16 + i]
                acc[2 * e + 1] -= x * turn_ref[32 + e * 16 + i]
        for e in range(2):
            re, im = acc[2 * e], acc[2 * e + 1]
            cos, sin = twid_ref[pl.ds(e, 1), :], twid_ref[pl.ds(2 + e, 1), :]
            held_ref[e, at, pl.ds(0, SPAN)] = re * cos + im * sin
            held_ref[e, at, pl.ds(SPAN, SPAN)] = im * cos - re * sin
        return _

    lax.fori_loop(0, rows // CHUNK, step, None)


def merge(held_ref, turn_ref, twid_ref, keep_ref, send_ref):
    rows = held_ref.shape[1]

    def step(n, _):
        at = pl.ds(pl.multiple_of(n * CHUNK, CHUNK), CHUNK)
        turned = []
        for e in range(2):
            re = held_ref[e, at, pl.ds(0, SPAN)] * (1.0 / FULL)
            im = held_ref[e, at, pl.ds(SPAN, SPAN)] * (1.0 / FULL)
            cos, sin = twid_ref[pl.ds(e, 1), :], twid_ref[pl.ds(2 + e, 1), :]
            turned.append((re * cos - im * sin, re * sin + im * cos))
        for i in range(16):
            total = jnp.zeros((CHUNK, SPAN), F32)
            for e in range(2):
                total += turned[e][0] * turn_ref[e * 16 + i]
                total -= turned[e][1] * turn_ref[32 + e * 16 + i]
            out = send_ref if i % 2 else keep_ref
            out[i // 2, at, :] = total.astype(out.dtype)
        return _

    lax.fori_loop(0, rows // CHUNK, step, None)


def dft(held, inner):
    return jnp.dot(held, inner, precision=HIGHEST, preferred_element_type=F32)


def idft(held, inner):
    return lax.dot_general(
        held, inner, (((1,), (1,)), ((), ())), precision=HIGHEST, preferred_element_type=F32
    )


def slot_list(refs):
    slots = {}
    for core in range(2):
        own, far, *pairs = refs[5 * core : 5 * core + 5]
        slots[core] = (own, None)
        slots[8 + core] = (far, None)
        for ky, pair in enumerate(pairs, 1):
            slots[2 * ky + core] = (pair, 0)
            slots[8 + 2 * ky + core] = (pair, 1)
    return [slots[i] for i in range(16)]


def forward_kernel(turn_ref, twid_ref, inner_ref, filt_ref, *refs):
    slot_refs = slot_list(refs[:10])
    freq_ref, keep_ref, send_ref, held_ref = refs[10:]
    spread(slot_refs, turn_ref, twid_ref, held_ref)
    for e in range(2):
        freq = dft(held_ref[e], inner_ref[...])
        freq_ref[e] = freq
        re, im = freq[:, :SPAN], freq[:, SPAN:]
        filt_re, filt_im = filt_ref[0, e], filt_ref[1, e]
        prod = jnp.concatenate([filt_re * re - filt_im * im, filt_re * im + filt_im * re], 1)
        held_ref[e] = idft(prod, inner_ref[...])
    merge(held_ref, turn_ref, twid_ref, keep_ref, send_ref)


def backward_kernel(turn_ref, twid_ref, inner_ref, filt_ref, sig_ref, *refs):
    slot_refs = slot_list(refs[:10])
    cross_ref, keep_ref, send_ref, held_ref = refs[10:]
    spread(slot_refs, turn_ref, twid_ref, held_ref)
    for e in range(2):
        freq = dft(held_ref[e], inner_ref[...])
        re, im = freq[:, :SPAN], freq[:, SPAN:]
        sig_re, sig_im = sig_ref[e, :, :SPAN], sig_ref[e, :, SPAN:]
        cross_ref[0, e] = (re * sig_re + im * sig_im) * (1.0 / FULL)
        cross_ref[1, e] = (im * sig_re - re * sig_im) * (1.0 / FULL)
        filt_re, filt_im = filt_ref[0, e], filt_ref[1, e]
        prod = jnp.concatenate([filt_re * re + filt_im * im, filt_re * im - filt_im * re], 1)
        held_ref[e] = idft(prod, inner_ref[...])
    merge(held_ref, turn_ref, twid_ref, keep_ref, send_ref)


PARAMS = pltpu.CompilerParams(vmem_limit_bytes=32 * 1024 * 1024)


def forward_call(consts, filt, blocks, send_type):
    rows = filt.shape[2]
    return pl.pallas_call(
        forward_kernel,
        out_shape=(
            jax.ShapeDtypeStruct((2, rows, 2 * SPAN), F32),
            jax.ShapeDtypeStruct((8, rows, SPAN), F32),
            jax.ShapeDtypeStruct((8, rows, SPAN), send_type),
        ),
        in_specs=[SMEM] + [VMEM] * 13,
        out_specs=(VMEM,) * 3,
        scratch_shapes=[pltpu.VMEM((2, rows, 2 * SPAN), F32)],
        compiler_params=PARAMS,
        cost_estimate=cost(2_000_000_000, 4 << 20),
        name="forward_transform",
    )(*consts, filt, *blocks)


def backward_call(consts, filt, sig_freq, blocks, send_type):
    rows = filt.shape[2]
    return pl.pallas_call(
        backward_kernel,
        out_shape=(
            jax.ShapeDtypeStruct((2, 2, rows, SPAN), F32),
            jax.ShapeDtypeStruct((8, rows, SPAN), F32),
            jax.ShapeDtypeStruct((8, rows, SPAN), send_type),
        ),
        in_specs=[SMEM] + [VMEM] * 14,
        out_specs=(VMEM,) * 3,
        scratch_shapes=[pltpu.VMEM((2, rows, 2 * SPAN), F32)],
        compiler_params=PARAMS,
        cost_estimate=cost(2_000_000_000, 4 << 20),
        name="backward_transform",
    )(*consts, filt, sig_freq, *blocks)


def weight_rows(weight_ref, place_ref, kx, kz, rows):
    start = (place_ref[0] ^ kz) * 4 + (place_ref[1] ^ kx)
    return weight_ref[pl.ds(pl.multiple_of(start * rows, rows), rows), :]


def partial_kernel(place_ref, weight_ref, cot_ref, *out_refs):
    rows = out_refs[0].shape[1]
    for kx in (2, 1, 3, 0):
        for kz in range(4):
            out_refs[kx][kz] = lax.dot_general(
                weight_rows(weight_ref, place_ref, kx, kz, rows),
                cot_ref[...],
                (((1,), (1,)), ((), ())),
                preferred_element_type=F32,
            ).astype(BF16)


def partial_call(place, weight, cot):
    rows = weight.shape[0] // N_CHAN
    return pl.pallas_call(
        partial_kernel,
        out_shape=(jax.ShapeDtypeStruct((4, rows, cot.shape[0]), BF16),) * 4,
        in_specs=[SMEM, VMEM, VMEM],
        out_specs=(VMEM,) * 4,
        compiler_params=PARAMS,
        cost_estimate=cost(268_000_000, 3 << 20),
        name="partial_grad_mixed",
    )(place, weight, cot)


def project_kernel(place_ref, weight_ref, *refs):
    out_ref = refs[-1]
    total = None
    for kx in range(4):
        for kz in range(4):
            block = refs[kx][kz]
            term = lax.dot_general(
                block,
                weight_rows(weight_ref, place_ref, kx, kz, block.shape[0]),
                (((0,), (0,)), ((), ())),
                preferred_element_type=F32,
            )
            total = term if total is None else total + term
    out_ref[...] = total.astype(BF16)


def project_call(place, weight, groups):
    return pl.pallas_call(
        project_kernel,
        out_shape=jax.ShapeDtypeStruct((SPAN, weight.shape[1]), BF16),
        in_specs=[SMEM] + [VMEM] * 5,
        out_specs=VMEM,
        compiler_params=PARAMS,
        cost_estimate=cost(268_000_000, 3 << 20),
        name="project_output",
    )(place, weight, *groups)


def gather_ctx(block):
    far = swap(block, "ctx", 8)
    both = jnp.stack([block, far])
    held = [block, far] + [swap(both, "ctx", 2 * ky) for ky in (1, 2, 3)]
    return held + [swap(part, "ctx", 1) for part in held]


def reduce_ctx(keep, send):
    keep = keep + swap(send, "ctx", 1).astype(F32)
    keep = keep.reshape(2, 4, *keep.shape[1:])
    pairs = [swap(keep[:, ky].astype(BF16), "ctx", 2 * ky) for ky in (1, 2, 3)]
    total = keep[:, 0]
    for pair in pairs:
        total = total + pair.astype(F32)
    return total[0] + swap(total[1].astype(BF16), "ctx", 8).astype(F32)


def reduce_chan(parts):
    total = parts[0].astype(F32)
    for kx in (1, 2, 3):
        total = total + swap(parts[kx], "chan", kx).astype(F32)
    result = total[0]
    for kz in (1, 2, 3):
        result = result + swap(total[kz].astype(BF16), "chan", 4 * kz).astype(F32)
    return result


def gather_chan(block):
    group = jnp.stack([block] + [swap(block, "chan", 4 * kz) for kz in (1, 2, 3)])
    return [group] + [swap(group, "chan", kx) for kx in (1, 2, 3)]


def body(signal, gating, skip_gain, spectrum, out_weight, cotangent):
    ctx = lax.axis_index("ctx")
    chan = lax.axis_index("chan")
    place = jnp.stack([chan // 4, chan % 4]).astype(jnp.int32)
    turn, twid, inner = tables()
    consts = (
        lax.dynamic_index_in_dim(turn, ctx, 0, keepdims=False),
        lax.dynamic_index_in_dim(twid, ctx, 0, keepdims=False),
        jnp.asarray(inner),
    )
    gate = gating.astype(F32)
    skip = skip_gain[:, None]
    filt = jnp.transpose(spectrum, (0, 2, 1, 3))

    parts = partial_call(place, out_weight, cotangent)
    sig_blocks = gather_ctx(signal)
    grad_mixed = reduce_chan(parts)
    grad_pre = (gate * grad_mixed).astype(BF16)

    sig_freq, conv_keep, conv_send = forward_call(consts, filt, sig_blocks, F32)
    pre_gate = reduce_ctx(conv_keep, conv_send) + skip * signal.astype(F32)
    mixed = (gate * pre_gate).astype(BF16)

    grad_blocks = gather_ctx(grad_pre)
    cross, back_keep, back_send = backward_call(consts, filt, sig_freq, grad_blocks, F32)
    grad_signal = (reduce_ctx(back_keep, back_send) + skip * grad_pre.astype(F32)).astype(BF16)

    output = project_call(place, out_weight, gather_chan(mixed))
    grad_gating = (grad_mixed * pre_gate).astype(BF16)
    return output, grad_signal, grad_gating, jnp.transpose(cross, (0, 2, 1, 3))


def solution(mesh):
    placed = (
        P("chan", "ctx"),
        P("chan", "ctx"),
        P("chan"),
        P(None, "chan", "ctx", None),
        P(None, "chan"),
        P("ctx", "chan"),
    )
    return jax.shard_map(
        body,
        mesh=mesh,
        in_specs=placed,
        out_specs=(
            P("ctx", "chan"),
            P("chan", "ctx"),
            P("chan", "ctx"),
            P(None, "chan", "ctx", None),
        ),
        check_vma=False,
    )
```

```python
import math

import jax
import jax.numpy as jnp
import numpy as np
from jax import lax
from jax.experimental import pallas as pl
from jax.experimental.pallas import tpu as pltpu
from jax.sharding import PartitionSpec as P

F32 = jnp.float32
BF16 = jnp.bfloat16
VMEM = pl.BlockSpec(memory_space=pltpu.VMEM)
SMEM = pl.BlockSpec(memory_space=pltpu.SMEM)

N_CTX = 16
N_CHAN = 16
SPAN = 128
FULL = 2 * N_CTX * SPAN


def swap(block, axis, mask):
    return lax.ppermute(block, axis, [(i, i ^ mask) for i in range(16)])


def rev4(number):
    return int(f"{number:04b}"[::-1], 2)


def phase(turns, modulus):
    angle = (turns % modulus) * (2.0 * math.pi / modulus)
    return np.cos(angle), np.sin(angle)


def tables():
    ranks = np.arange(N_CTX)
    residues = np.array([[2 * rev4(r ^ 8 * far) + e for far in range(2) for e in range(2)] for r in ranks])
    slots = ranks[:, None] ^ ranks[None, :]
    turn = np.stack(phase(slots[:, None, :] * residues[:, :, None], 32), 1)
    twid = np.stack(phase(residues[:, :, None] * np.arange(SPAN), FULL), 1)
    cos, sin = phase(np.arange(SPAN)[:, None] * np.arange(SPAN), SPAN)
    inner = np.block([[cos, -sin], [sin, cos]]).astype(np.float32)
    high = inner.astype(jnp.bfloat16)
    low = (inner - high.astype(np.float32)).astype(jnp.bfloat16)
    return (
        turn.reshape(N_CTX, 2 * RES * 16).astype(np.float32),
        twid.reshape(N_CTX, 2 * RES, SPAN).astype(np.float32),
        np.stack([high, low]),
    )


def fence(*values):
    return lax.optimization_barrier(values)


def cost(flops, moved):
    return pl.CostEstimate(flops=flops, bytes_accessed=moved, transcendentals=0)


CHUNK = 32
RES = 4


def spread(slot_refs, turn_ref, twid_ref, held_ref):
    rows = held_ref.shape[1]

    def step(n, _):
        at = pl.ds(pl.multiple_of(n * CHUNK, CHUNK), CHUNK)
        acc = [None] * (2 * RES)
        for i, (ref, place) in enumerate(slot_refs):
            x = (ref[at, :] if place is None else ref[place, at, :]).astype(F32)
            for e in range(2 * RES):
                term = x * turn_ref[e * 16 + i]
                acc[e] = term if acc[e] is None else acc[e] + term
        for e in range(RES):
            re, im = acc[e], acc[RES + e]
            cos, sin = twid_ref[pl.ds(e, 1), :], twid_ref[pl.ds(RES + e, 1), :]
            held_ref[e, at, pl.ds(0, SPAN)] = re * cos - im * sin
            held_ref[e, at, pl.ds(SPAN, SPAN)] = -(im * cos + re * sin)
        return _

    lax.fori_loop(0, rows // CHUNK, step, None)


def merge(held_ref, turn_ref, twid_ref, keep_ref, send_ref):
    rows = held_ref.shape[1]

    def step(n, _):
        at = pl.ds(pl.multiple_of(n * CHUNK, CHUNK), CHUNK)
        turned = []
        for e in range(RES):
            re = held_ref[e, at, pl.ds(0, SPAN)] * (1.0 / FULL)
            im = held_ref[e, at, pl.ds(SPAN, SPAN)] * (1.0 / FULL)
            cos, sin = twid_ref[pl.ds(e, 1), :], twid_ref[pl.ds(RES + e, 1), :]
            turned.append((re * cos - im * sin, re * sin + im * cos))
        for i in range(8):
            total = None
            for e in range(RES):
                term = turned[e][0] * turn_ref[e * 16 + i] - turned[e][1] * turn_ref[(RES + e) * 16 + i]
                total = term if total is None else total + term
            out = send_ref if i % 2 else keep_ref
            out[i // 2, at, :] = total
        return _

    lax.fori_loop(0, rows // CHUNK, step, None)


def dft(held, inner_ref, contract):
    high = held.astype(BF16)
    low = (held - high.astype(F32)).astype(BF16)

    def dot(x, y):
        return lax.dot_general(x, y, (((1,), (contract,)), ((), ())), preferred_element_type=F32)

    return dot(high, inner_ref[0]) + (dot(low, inner_ref[0]) + dot(high, inner_ref[1]))


def slot_list(refs):
    slots = {}
    for core in range(2):
        own, far, *pairs = refs[5 * core : 5 * core + 5]
        slots[core] = (own, None)
        slots[8 + core] = (far, None)
        for ky, pair in enumerate(pairs, 1):
            slots[2 * ky + core] = (pair, 0)
            slots[8 + 2 * ky + core] = (pair, 1)
    return [slots[i] for i in range(16)]


def filters(filt_ref, far_ref, e):
    if e < 2:
        return filt_ref[0, e], filt_ref[1, e]
    return far_ref[0, e - 2].astype(F32), far_ref[1, e - 2].astype(F32)


def forward_kernel(turn_ref, twid_ref, inner_ref, filt_ref, far_ref, *refs):
    slot_refs = slot_list(refs[:10])
    freq_ref, keep_ref, send_ref, held_ref = refs[10:]
    spread(slot_refs, turn_ref, twid_ref, held_ref)
    for e in range(RES):
        freq = dft(held_ref[e], inner_ref, 0)
        if e < 2:
            freq_ref[e] = freq
        re, im = freq[:, :SPAN], freq[:, SPAN:]
        filt_re, filt_im = filters(filt_ref, far_ref, e)
        prod = jnp.concatenate([filt_re * re - filt_im * im, filt_re * im + filt_im * re], 1)
        held_ref[e] = dft(prod, inner_ref, 1)
    merge(held_ref, turn_ref, twid_ref, keep_ref, send_ref)


def backward_kernel(turn_ref, twid_ref, inner_ref, filt_ref, far_ref, sig_ref, *refs):
    slot_refs = slot_list(refs[:10])
    cross_ref, keep_ref, send_ref, held_ref = refs[10:]
    spread(slot_refs, turn_ref, twid_ref, held_ref)
    for e in range(RES):
        freq = dft(held_ref[e], inner_ref, 0)
        re, im = freq[:, :SPAN], freq[:, SPAN:]
        if e < 2:
            sig_re, sig_im = sig_ref[e, :, :SPAN], sig_ref[e, :, SPAN:]
            cross_ref[0, e] = (re * sig_re + im * sig_im) * (1.0 / FULL)
            cross_ref[1, e] = (im * sig_re - re * sig_im) * (1.0 / FULL)
        filt_re, filt_im = filters(filt_ref, far_ref, e)
        prod = jnp.concatenate([filt_re * re + filt_im * im, filt_re * im - filt_im * re], 1)
        held_ref[e] = dft(prod, inner_ref, 1)
    merge(held_ref, turn_ref, twid_ref, keep_ref, send_ref)


PARAMS = pltpu.CompilerParams(vmem_limit_bytes=32 * 1024 * 1024)


def transform_call(kernel, name, kept, consts, filt, far, extra, blocks):
    rows = filt.shape[2]
    operands = (*consts, filt, far, *extra, *blocks)
    return pl.pallas_call(
        kernel,
        out_shape=(
            kept,
            jax.ShapeDtypeStruct((4, rows, SPAN), F32),
            jax.ShapeDtypeStruct((4, rows, SPAN), F32),
        ),
        in_specs=[SMEM] + [VMEM] * (len(operands) - 1),
        out_specs=(VMEM,) * 3,
        scratch_shapes=[pltpu.VMEM((RES, rows, 2 * SPAN), F32)],
        compiler_params=PARAMS,
        cost_estimate=cost(2_000_000_000, 4 << 20),
        name=name,
    )(*operands)


def forward_call(consts, filt, far, blocks):
    kept = jax.ShapeDtypeStruct((2, filt.shape[2], 2 * SPAN), F32)
    return transform_call(forward_kernel, "forward_transform", kept, consts, filt, far, (), blocks)


def backward_call(consts, filt, far, sig_freq, blocks):
    kept = jax.ShapeDtypeStruct(filt.shape, F32)
    return transform_call(
        backward_kernel, "backward_transform", kept, consts, filt, far, (sig_freq,), blocks
    )


def fold_kernel(*refs):
    *in_refs, own_ref, a_ref, b_ref, c_ref = refs
    for k, out in enumerate((own_ref, a_ref, b_ref, c_ref)):
        total = in_refs[0][k].astype(F32)
        for ref in in_refs[1:]:
            total = total + ref[k].astype(F32)
        out[...] = total.astype(out.dtype)


def fold_call(*parts):
    block = parts[0].shape[1:]
    return pl.pallas_call(
        fold_kernel,
        out_shape=(jax.ShapeDtypeStruct(block, F32),) + (jax.ShapeDtypeStruct(block, BF16),) * 3,
        in_specs=[VMEM] * len(parts),
        out_specs=(VMEM,) * 4,
        compiler_params=PARAMS,
        cost_estimate=cost(1 << 20, 2 << 20),
        name="fold",
    )(*parts)


def weight_rows(weight_ref, place_ref, kx, kz, rows):
    start = (place_ref[0] ^ kz) * 4 + (place_ref[1] ^ kx)
    return weight_ref[pl.ds(pl.multiple_of(start * rows, rows), rows), :]


def partial_kernel(place_ref, weight_ref, cot_ref, *out_refs):
    rows = out_refs[0].shape[1]
    for kx in (2, 1, 3, 0):
        for kz in range(4):
            out_refs[kx][kz] = lax.dot_general(
                weight_rows(weight_ref, place_ref, kx, kz, rows),
                cot_ref[...],
                (((1,), (1,)), ((), ())),
                preferred_element_type=F32,
            ).astype(BF16)


def partial_call(place, weight, cot):
    rows = weight.shape[0] // N_CHAN
    return pl.pallas_call(
        partial_kernel,
        out_shape=(jax.ShapeDtypeStruct((4, rows, cot.shape[0]), BF16),) * 4,
        in_specs=[SMEM, VMEM, VMEM],
        out_specs=(VMEM,) * 4,
        compiler_params=PARAMS,
        cost_estimate=cost(268_000_000, 3 << 20),
        name="partial_grad_mixed",
    )(place, weight, cot)


def project_kernel(place_ref, weight_ref, *refs):
    out_ref = refs[-1]
    total = None
    for kx in range(4):
        for kz in range(4):
            block = refs[kx][kz]
            term = lax.dot_general(
                block,
                weight_rows(weight_ref, place_ref, kx, kz, block.shape[0]),
                (((0,), (0,)), ((), ())),
                preferred_element_type=F32,
            )
            total = term if total is None else total + term
    out_ref[...] = total.astype(BF16)


def project_call(place, weight, groups):
    return pl.pallas_call(
        project_kernel,
        out_shape=jax.ShapeDtypeStruct((SPAN, weight.shape[1]), BF16),
        in_specs=[SMEM] + [VMEM] * 5,
        out_specs=VMEM,
        compiler_params=PARAMS,
        cost_estimate=cost(268_000_000, 3 << 20),
        name="project_output",
    )(place, weight, *groups)


def gather_ctx(block):
    far = swap(block, "ctx", 8)
    both = jnp.stack([block, far])
    held = [block, far] + [swap(both, "ctx", 2 * ky) for ky in (1, 2, 3)]
    return held + [swap(part, "ctx", 1) for part in held]


def reduce_ctx(keep, send):
    own, *parts = fold_call(keep, swap(send, "ctx", 1))
    for ky, part in enumerate(parts, 1):
        own = own + swap(part, "ctx", 2 * ky).astype(F32)
    return own


def reduce_chan(parts):
    own, *parts = fold_call(parts[0], *[swap(parts[kx], "chan", kx) for kx in (1, 2, 3)])
    for kz, part in enumerate(parts, 1):
        own = own + swap(part, "chan", 4 * kz).astype(F32)
    return own


def gather_chan(block):
    group = jnp.stack([block] + [swap(block, "chan", 4 * kz) for kz in (1, 2, 3)])
    return [group] + [swap(group, "chan", kx) for kx in (1, 2, 3)]


def body(signal, gating, skip_gain, spectrum, out_weight, cotangent):
    ctx = lax.axis_index("ctx")
    chan = lax.axis_index("chan")
    place = jnp.stack([chan // 4, chan % 4]).astype(jnp.int32)
    turn, twid, inner = tables()
    consts = (
        lax.dynamic_index_in_dim(turn, ctx, 0, keepdims=False),
        lax.dynamic_index_in_dim(twid, ctx, 0, keepdims=False),
        jnp.asarray(inner),
    )
    gate = gating.astype(F32)
    skip = skip_gain[:, None]
    filt = jnp.transpose(spectrum, (0, 2, 1, 3))

    sig_far = swap(signal, "ctx", 8)
    far = swap(filt.astype(BF16), "ctx", 8)
    parts = partial_call(place, out_weight, cotangent)
    folded = fold_call(parts[0], *[swap(parts[kx], "chan", kx) for kx in (1, 2, 3)])
    far, folded = fence(far, folded)
    both = jnp.stack([signal, sig_far])
    held = [signal, sig_far] + [swap(both, "ctx", 2 * ky) for ky in (1, 2, 3)]
    sig_blocks = held + [swap(part, "ctx", 1) for part in held]
    grad_mixed, *rest = folded
    for kz, part in enumerate(rest, 1):
        grad_mixed = grad_mixed + swap(part, "chan", 4 * kz).astype(F32)
    grad_pre = (gate * grad_mixed).astype(BF16)
    sig_blocks, grad_pre = fence(sig_blocks, grad_pre)
    grad_far = swap(grad_pre, "ctx", 8)

    sig_freq, conv_keep, conv_send = forward_call(consts, filt, far, sig_blocks)
    conv_keep, conv_send, grad_far = fence(conv_keep, conv_send, grad_far)
    conv = fold_call(conv_keep, swap(conv_send, "ctx", 1))
    conv, grad_far = fence(conv, grad_far)

    conv_own, *rest = conv
    for ky, part in enumerate(rest, 1):
        conv_own = conv_own + swap(part, "ctx", 2 * ky).astype(F32)
    pre_gate = conv_own + skip * signal.astype(F32)
    mixed = (gate * pre_gate).astype(BF16)
    both = jnp.stack([grad_pre, grad_far])
    held = [grad_pre, grad_far] + [swap(both, "ctx", 2 * ky) for ky in (1, 2, 3)]
    mixed, held = fence(mixed, held)

    group = jnp.stack([mixed] + [swap(mixed, "chan", 4 * kz) for kz in (1, 2, 3)])
    grad_blocks = held + [swap(part, "ctx", 1) for part in held]
    cross, back_keep, back_send = backward_call(consts, filt, far, sig_freq, grad_blocks)
    group, back_keep, back_send = fence(group, back_keep, back_send)
    back = fold_call(back_keep, swap(back_send, "ctx", 1))
    groups = [group] + [swap(group, "chan", kx) for kx in (1, 2, 3)]
    back_own, *rest = back
    for ky, part in enumerate(rest, 1):
        back_own = back_own + swap(part, "ctx", 2 * ky).astype(F32)
    grad_signal = (back_own + skip * grad_pre.astype(F32)).astype(BF16)
    output = project_call(place, out_weight, groups)
    grad_gating = (grad_mixed * pre_gate).astype(BF16)
    return output, grad_signal, grad_gating, jnp.transpose(cross, (0, 2, 1, 3))


def solution(mesh):
    placed = (
        P("chan", "ctx"),
        P("chan", "ctx"),
        P("chan"),
        P(None, "chan", "ctx", None),
        P(None, "chan"),
        P("ctx", "chan"),
    )
    return jax.shard_map(
        body,
        mesh=mesh,
        in_specs=placed,
        out_specs=(
            P("ctx", "chan"),
            P("chan", "ctx"),
            P("chan", "ctx"),
            P(None, "chan", "ctx", None),
        ),
        check_vma=False,
    )
```

```python
import math

import jax
import jax.numpy as jnp
import numpy as np
from jax import lax
from jax.experimental import pallas as pl
from jax.experimental.pallas import tpu as pltpu
from jax.sharding import PartitionSpec as P

F32 = jnp.float32
BF16 = jnp.bfloat16
VMEM = pl.BlockSpec(memory_space=pltpu.VMEM)
SMEM = pl.BlockSpec(memory_space=pltpu.SMEM)

N_CTX = 16
N_CHAN = 16
SPAN = 128
FULL = 2 * N_CTX * SPAN


def swap(block, axis, mask):
    return lax.ppermute(block, axis, [(i, i ^ mask) for i in range(16)])


def rev4(number):
    return int(f"{number:04b}"[::-1], 2)


def phase(turns, modulus):
    angle = (turns % modulus) * (2.0 * math.pi / modulus)
    return np.cos(angle), np.sin(angle)


def tables():
    ranks = np.arange(N_CTX)
    residues = np.array([[2 * rev4(r ^ 8 * far) + e for far in range(2) for e in range(2)] for r in ranks])
    slots = ranks[:, None] ^ ranks[None, :]
    turn = np.stack(phase(slots[:, None, :] * residues[:, :, None], 32), 1)
    twid = np.stack(phase(residues[:, :, None] * np.arange(SPAN), FULL), 1)
    cos, sin = phase(np.arange(SPAN)[:, None] * np.arange(SPAN), SPAN)
    inner = np.block([[cos, -sin], [sin, cos]]).astype(np.float32)
    high = inner.astype(jnp.bfloat16)
    low = (inner - high.astype(np.float32)).astype(jnp.bfloat16)
    return (
        turn.reshape(N_CTX, 2 * RES * 16).astype(np.float32),
        twid.reshape(N_CTX, 2 * RES, SPAN).astype(np.float32),
        np.stack([high, low]),
    )


def fence(*values):
    return lax.optimization_barrier(values)


def cost(flops, moved):
    return pl.CostEstimate(flops=flops, bytes_accessed=moved, transcendentals=0)


CHUNK = 32
RES = 4


def spread(slot_refs, turn_ref, twid_ref, held_ref):
    rows = held_ref.shape[1]

    def step(n, _):
        at = pl.ds(pl.multiple_of(n * CHUNK, CHUNK), CHUNK)
        acc = [None] * (2 * RES)
        for i, (ref, place) in enumerate(slot_refs):
            x = (ref[at, :] if place is None else ref[place, at, :]).astype(F32)
            for e in range(2 * RES):
                term = x * turn_ref[e * 16 + i]
                acc[e] = term if acc[e] is None else acc[e] + term
        for e in range(RES):
            re, im = acc[e], acc[RES + e]
            cos, sin = twid_ref[pl.ds(e, 1), :], twid_ref[pl.ds(RES + e, 1), :]
            held_ref[e, at, pl.ds(0, SPAN)] = re * cos - im * sin
            held_ref[e, at, pl.ds(SPAN, SPAN)] = -(im * cos + re * sin)
        return _

    lax.fori_loop(0, rows // CHUNK, step, None)


def merge(held_ref, turn_ref, twid_ref, keep_ref, send_ref):
    rows = held_ref.shape[1]

    def step(n, _):
        at = pl.ds(pl.multiple_of(n * CHUNK, CHUNK), CHUNK)
        turned = []
        for e in range(RES):
            re = held_ref[e, at, pl.ds(0, SPAN)] * (1.0 / FULL)
            im = held_ref[e, at, pl.ds(SPAN, SPAN)] * (1.0 / FULL)
            cos, sin = twid_ref[pl.ds(e, 1), :], twid_ref[pl.ds(RES + e, 1), :]
            turned.append((re * cos - im * sin, re * sin + im * cos))
        for i in range(8):
            total = None
            for e in range(RES):
                term = turned[e][0] * turn_ref[e * 16 + i] - turned[e][1] * turn_ref[(RES + e) * 16 + i]
                total = term if total is None else total + term
            out = send_ref if i % 2 else keep_ref
            out[i // 2, at, :] = total
        return _

    lax.fori_loop(0, rows // CHUNK, step, None)


def dft(held, inner_ref, contract):
    high = held.astype(BF16)
    low = (held - high.astype(F32)).astype(BF16)

    def dot(x, y):
        return lax.dot_general(x, y, (((1,), (contract,)), ((), ())), preferred_element_type=F32)

    return dot(high, inner_ref[0]) + (dot(low, inner_ref[0]) + dot(high, inner_ref[1]))


def slot_list(refs):
    slots = {}
    for core in range(2):
        own, far, *pairs = refs[5 * core : 5 * core + 5]
        slots[core] = (own, None)
        slots[8 + core] = (far, None)
        for ky, pair in enumerate(pairs, 1):
            slots[2 * ky + core] = (pair, 0)
            slots[8 + 2 * ky + core] = (pair, 1)
    return [slots[i] for i in range(16)]


def filters(filt_ref, far_ref, e):
    if e < 2:
        return filt_ref[0, e], filt_ref[1, e]
    return far_ref[0, e - 2].astype(F32), far_ref[1, e - 2].astype(F32)


def forward_kernel(turn_ref, twid_ref, inner_ref, filt_ref, far_ref, *refs):
    slot_refs = slot_list(refs[:10])
    freq_ref, keep_ref, send_ref, held_ref = refs[10:]
    spread(slot_refs, turn_ref, twid_ref, held_ref)
    for e in range(RES):
        freq = dft(held_ref[e], inner_ref, 0)
        if e < 2:
            freq_ref[e] = freq
        re, im = freq[:, :SPAN], freq[:, SPAN:]
        filt_re, filt_im = filters(filt_ref, far_ref, e)
        prod = jnp.concatenate([filt_re * re - filt_im * im, filt_re * im + filt_im * re], 1)
        held_ref[e] = dft(prod, inner_ref, 1)
    merge(held_ref, turn_ref, twid_ref, keep_ref, send_ref)


def backward_kernel(turn_ref, twid_ref, inner_ref, filt_ref, far_ref, sig_ref, *refs):
    slot_refs = slot_list(refs[:10])
    cross_ref, keep_ref, send_ref, held_ref = refs[10:]
    spread(slot_refs, turn_ref, twid_ref, held_ref)
    for e in range(RES):
        freq = dft(held_ref[e], inner_ref, 0)
        re, im = freq[:, :SPAN], freq[:, SPAN:]
        if e < 2:
            sig_re, sig_im = sig_ref[e, :, :SPAN], sig_ref[e, :, SPAN:]
            cross_ref[0, e] = (re * sig_re + im * sig_im) * (1.0 / FULL)
            cross_ref[1, e] = (im * sig_re - re * sig_im) * (1.0 / FULL)
        filt_re, filt_im = filters(filt_ref, far_ref, e)
        prod = jnp.concatenate([filt_re * re + filt_im * im, filt_re * im - filt_im * re], 1)
        held_ref[e] = dft(prod, inner_ref, 1)
    merge(held_ref, turn_ref, twid_ref, keep_ref, send_ref)


PARAMS = pltpu.CompilerParams(vmem_limit_bytes=32 * 1024 * 1024)


def transform_call(kernel, name, kept, consts, filt, far, extra, blocks):
    rows = filt.shape[2]
    operands = (*consts, filt, far, *extra, *blocks)
    return pl.pallas_call(
        kernel,
        out_shape=(
            kept,
            jax.ShapeDtypeStruct((4, rows, SPAN), F32),
            jax.ShapeDtypeStruct((4, rows, SPAN), F32),
        ),
        in_specs=[SMEM] + [VMEM] * (len(operands) - 1),
        out_specs=(VMEM,) * 3,
        scratch_shapes=[pltpu.VMEM((RES, rows, 2 * SPAN), F32)],
        compiler_params=PARAMS,
        cost_estimate=cost(2_000_000_000, 4 << 20),
        name=name,
    )(*operands)


def forward_call(consts, filt, far, blocks):
    kept = jax.ShapeDtypeStruct((2, filt.shape[2], 2 * SPAN), F32)
    return transform_call(forward_kernel, "forward_transform", kept, consts, filt, far, (), blocks)


def backward_call(consts, filt, far, sig_freq, blocks):
    kept = jax.ShapeDtypeStruct(filt.shape, F32)
    return transform_call(
        backward_kernel, "backward_transform", kept, consts, filt, far, (sig_freq,), blocks
    )


def fold_kernel(*refs):
    *in_refs, own_ref, a_ref, b_ref, c_ref = refs
    for k, out in enumerate((own_ref, a_ref, b_ref, c_ref)):
        total = in_refs[0][k].astype(F32)
        for ref in in_refs[1:]:
            total = total + ref[k].astype(F32)
        out[...] = total.astype(out.dtype)


def fold_call(*parts):
    block = parts[0].shape[1:]
    return pl.pallas_call(
        fold_kernel,
        out_shape=(jax.ShapeDtypeStruct(block, F32),) + (jax.ShapeDtypeStruct(block, BF16),) * 3,
        in_specs=[VMEM] * len(parts),
        out_specs=(VMEM,) * 4,
        compiler_params=PARAMS,
        cost_estimate=cost(1 << 20, 2 << 20),
        name="fold",
    )(*parts)


def weight_rows(weight_ref, place_ref, kx, kz, rows):
    start = (place_ref[0] ^ kz) * 4 + (place_ref[1] ^ kx)
    return weight_ref[pl.ds(pl.multiple_of(start * rows, rows), rows), :]


def partial_kernel(place_ref, weight_ref, cot_ref, *out_refs):
    rows = out_refs[0].shape[1]
    for kx in (2, 1, 3, 0):
        for kz in range(4):
            out_refs[kx][kz] = lax.dot_general(
                weight_rows(weight_ref, place_ref, kx, kz, rows),
                cot_ref[...],
                (((1,), (1,)), ((), ())),
                preferred_element_type=F32,
            ).astype(BF16)


def partial_call(place, weight, cot):
    rows = weight.shape[0] // N_CHAN
    return pl.pallas_call(
        partial_kernel,
        out_shape=(jax.ShapeDtypeStruct((4, rows, cot.shape[0]), BF16),) * 4,
        in_specs=[SMEM, VMEM, VMEM],
        out_specs=(VMEM,) * 4,
        compiler_params=PARAMS,
        cost_estimate=cost(268_000_000, 3 << 20),
        name="partial_grad_mixed",
    )(place, weight, cot)


def project_kernel(place_ref, weight_ref, *refs):
    out_ref = refs[-1]
    total = None
    for kx in range(4):
        for kz in range(4):
            block = refs[kx][kz]
            term = lax.dot_general(
                block,
                weight_rows(weight_ref, place_ref, kx, kz, block.shape[0]),
                (((0,), (0,)), ((), ())),
                preferred_element_type=F32,
            )
            total = term if total is None else total + term
    out_ref[...] = total.astype(BF16)


def project_call(place, weight, groups):
    return pl.pallas_call(
        project_kernel,
        out_shape=jax.ShapeDtypeStruct((SPAN, weight.shape[1]), BF16),
        in_specs=[SMEM] + [VMEM] * 5,
        out_specs=VMEM,
        compiler_params=PARAMS,
        cost_estimate=cost(268_000_000, 3 << 20),
        name="project_output",
    )(place, weight, *groups)


def gather_ctx(block):
    far = swap(block, "ctx", 8)
    both = jnp.stack([block, far])
    held = [block, far] + [swap(both, "ctx", 2 * ky) for ky in (1, 2, 3)]
    return held + [swap(part, "ctx", 1) for part in held]


def reduce_ctx(keep, send):
    own, *parts = fold_call(keep, swap(send, "ctx", 1))
    for ky, part in enumerate(parts, 1):
        own = own + swap(part, "ctx", 2 * ky).astype(F32)
    return own


def reduce_chan(parts):
    own, *parts = fold_call(parts[0], *[swap(parts[kx], "chan", kx) for kx in (1, 2, 3)])
    for kz, part in enumerate(parts, 1):
        own = own + swap(part, "chan", 4 * kz).astype(F32)
    return own


def gather_chan(block):
    group = jnp.stack([block] + [swap(block, "chan", 4 * kz) for kz in (1, 2, 3)])
    return [group] + [swap(group, "chan", kx) for kx in (1, 2, 3)]


def body(signal, gating, skip_gain, spectrum, out_weight, cotangent):
    ctx = lax.axis_index("ctx")
    chan = lax.axis_index("chan")
    place = jnp.stack([chan // 4, chan % 4]).astype(jnp.int32)
    turn, twid, inner = tables()
    consts = (
        lax.dynamic_index_in_dim(turn, ctx, 0, keepdims=False),
        lax.dynamic_index_in_dim(twid, ctx, 0, keepdims=False),
        jnp.asarray(inner),
    )
    gate = gating.astype(F32)
    skip = skip_gain[:, None]
    filt = jnp.transpose(spectrum, (0, 2, 1, 3))

    sig_far = swap(signal, "ctx", 8)
    far = swap(filt.astype(BF16), "ctx", 8)
    parts = partial_call(place, out_weight, cotangent)
    got = [swap(parts[kx], "chan", kx) for kx in (1, 2, 3)]
    got[0], got[2], sig_far = fence(got[0], got[2], sig_far)
    folded = fold_call(parts[0], *got)
    both = jnp.stack([signal, sig_far])
    held = [signal, sig_far] + [swap(both, "ctx", 2 * ky) for ky in (1, 2, 3)]
    held, far = fence(held, far)
    sig_blocks = held + [swap(part, "ctx", 1) for part in held]
    grad_mixed, *rest = folded
    for kz, part in enumerate(rest, 1):
        grad_mixed = grad_mixed + swap(part, "chan", 4 * kz).astype(F32)
    grad_pre = (gate * grad_mixed).astype(BF16)
    sig_blocks, grad_pre = fence(sig_blocks, grad_pre)
    grad_far = swap(grad_pre, "ctx", 8)

    sig_freq, conv_keep, conv_send = forward_call(consts, filt, far, sig_blocks)
    conv_keep, conv_send, grad_far = fence(conv_keep, conv_send, grad_far)
    conv = fold_call(conv_keep, swap(conv_send, "ctx", 1))

    conv_own, *rest = conv
    for ky, part in enumerate(rest, 1):
        conv_own = conv_own + swap(part, "ctx", 2 * ky).astype(F32)
    pre_gate = conv_own + skip * signal.astype(F32)
    mixed = (gate * pre_gate).astype(BF16)
    both = jnp.stack([grad_pre, grad_far])
    held = [grad_pre, grad_far] + [swap(both, "ctx", 2 * ky) for ky in (1, 2, 3)]

    group = jnp.stack([mixed] + [swap(mixed, "chan", 4 * kz) for kz in (1, 2, 3)])
    grad_blocks = held + [swap(part, "ctx", 1) for part in held]
    cross, back_keep, back_send = backward_call(consts, filt, far, sig_freq, grad_blocks)
    group, back_keep, back_send = fence(group, back_keep, back_send)
    back = fold_call(back_keep, swap(back_send, "ctx", 1))
    groups = [group] + [swap(group, "chan", kx) for kx in (1, 2, 3)]
    back_own, *rest = back
    for ky, part in enumerate(rest, 1):
        back_own = back_own + swap(part, "ctx", 2 * ky).astype(F32)
    grad_signal = (back_own + skip * grad_pre.astype(F32)).astype(BF16)
    output = project_call(place, out_weight, groups)
    grad_gating = (grad_mixed * pre_gate).astype(BF16)
    return output, grad_signal, grad_gating, jnp.transpose(cross, (0, 2, 1, 3))


def solution(mesh):
    placed = (
        P("chan", "ctx"),
        P("chan", "ctx"),
        P("chan"),
        P(None, "chan", "ctx", None),
        P(None, "chan"),
        P("ctx", "chan"),
    )
    return jax.shard_map(
        body,
        mesh=mesh,
        in_specs=placed,
        out_specs=(
            P("ctx", "chan"),
            P("chan", "ctx"),
            P("chan", "ctx"),
            P(None, "chan", "ctx", None),
        ),
        check_vma=False,
    )
```

```python
import math

import jax
import jax.numpy as jnp
import numpy as np
from jax import lax
from jax.experimental import pallas as pl
from jax.experimental.pallas import tpu as pltpu
from jax.sharding import PartitionSpec as P

F32 = jnp.float32
BF16 = jnp.bfloat16
VMEM = pl.BlockSpec(memory_space=pltpu.VMEM)
SMEM = pl.BlockSpec(memory_space=pltpu.SMEM)

N_CTX = 16
N_CHAN = 16
SPAN = 128
FULL = 2 * N_CTX * SPAN


def swap(block, axis, mask):
    return lax.ppermute(block, axis, [(i, i ^ mask) for i in range(16)])


def rev4(number):
    return int(f"{number:04b}"[::-1], 2)


def phase(turns, modulus):
    angle = (turns % modulus) * (2.0 * math.pi / modulus)
    return np.cos(angle), np.sin(angle)


def tables():
    ranks = np.arange(N_CTX)
    residues = np.array([[2 * rev4(r ^ 8 * far) + e for far in range(2) for e in range(2)] for r in ranks])
    slots = ranks[:, None] ^ ranks[None, :]
    turn = np.stack(phase(slots[:, None, :] * residues[:, :, None], 32), 1)
    twid = np.stack(phase(residues[:, :, None] * np.arange(SPAN), FULL), 1)
    cos, sin = phase(np.arange(SPAN)[:, None] * np.arange(SPAN), SPAN)
    inner = np.block([[cos, -sin], [sin, cos]]).astype(np.float32)
    high = inner.astype(jnp.bfloat16)
    low = (inner - high.astype(np.float32)).astype(jnp.bfloat16)
    return (
        turn.reshape(N_CTX, 2 * RES * 16).astype(np.float32),
        twid.reshape(N_CTX, 2 * RES, SPAN).astype(np.float32),
        np.stack([high, low]),
    )


def fence(*values):
    return lax.optimization_barrier(values)


def cost(flops, moved):
    return pl.CostEstimate(flops=flops, bytes_accessed=moved, transcendentals=0)


CHUNK = 32
RES = 4


def spread(slot_refs, turn_ref, twid_ref, held_ref):
    rows = held_ref.shape[1]

    def step(n, _):
        at = pl.ds(pl.multiple_of(n * CHUNK, CHUNK), CHUNK)
        acc = [None] * (2 * RES)
        for i, (ref, place) in enumerate(slot_refs):
            x = (ref[at, :] if place is None else ref[place, at, :]).astype(F32)
            for e in range(2 * RES):
                term = x * turn_ref[e * 16 + i]
                acc[e] = term if acc[e] is None else acc[e] + term
        for e in range(RES):
            re, im = acc[e], acc[RES + e]
            cos, sin = twid_ref[pl.ds(e, 1), :], twid_ref[pl.ds(RES + e, 1), :]
            held_ref[e, at, pl.ds(0, SPAN)] = re * cos - im * sin
            held_ref[e, at, pl.ds(SPAN, SPAN)] = -(im * cos + re * sin)
        return _

    lax.fori_loop(0, rows // CHUNK, step, None)


def merge(held_ref, turn_ref, twid_ref, keep_ref, send_ref):
    rows = held_ref.shape[1]

    def step(n, _):
        at = pl.ds(pl.multiple_of(n * CHUNK, CHUNK), CHUNK)
        turned = []
        for e in range(RES):
            re = held_ref[e, at, pl.ds(0, SPAN)] * (1.0 / FULL)
            im = held_ref[e, at, pl.ds(SPAN, SPAN)] * (1.0 / FULL)
            cos, sin = twid_ref[pl.ds(e, 1), :], twid_ref[pl.ds(RES + e, 1), :]
            turned.append((re * cos - im * sin, re * sin + im * cos))
        for i in range(8):
            total = None
            for e in range(RES):
                term = turned[e][0] * turn_ref[e * 16 + i] - turned[e][1] * turn_ref[(RES + e) * 16 + i]
                total = term if total is None else total + term
            out = send_ref if i % 2 else keep_ref
            out[i // 2, at, :] = total
        return _

    lax.fori_loop(0, rows // CHUNK, step, None)


def dft(held, inner_ref, contract):
    high = held.astype(BF16)
    low = (held - high.astype(F32)).astype(BF16)

    def dot(x, y):
        return lax.dot_general(x, y, (((1,), (contract,)), ((), ())), preferred_element_type=F32)

    return dot(high, inner_ref[0]) + (dot(low, inner_ref[0]) + dot(high, inner_ref[1]))


def slot_list(refs):
    slots = {}
    for core in range(2):
        own, far, *pairs = refs[5 * core : 5 * core + 5]
        slots[core] = (own, None)
        slots[8 + core] = (far, None)
        for ky, pair in enumerate(pairs, 1):
            slots[2 * ky + core] = (pair, 0)
            slots[8 + 2 * ky + core] = (pair, 1)
    return [slots[i] for i in range(16)]


def filters(filt_ref, far_ref, e):
    if e < 2:
        return filt_ref[0, e], filt_ref[1, e]
    return far_ref[0, e - 2].astype(F32), far_ref[1, e - 2].astype(F32)


def forward_kernel(turn_ref, twid_ref, inner_ref, filt_ref, far_ref, *refs):
    slot_refs = slot_list(refs[:10])
    freq_ref, keep_ref, send_ref, held_ref = refs[10:]
    spread(slot_refs, turn_ref, twid_ref, held_ref)
    for e in range(RES):
        freq = dft(held_ref[e], inner_ref, 0)
        if e < 2:
            freq_ref[e] = freq
        re, im = freq[:, :SPAN], freq[:, SPAN:]
        filt_re, filt_im = filters(filt_ref, far_ref, e)
        prod = jnp.concatenate([filt_re * re - filt_im * im, filt_re * im + filt_im * re], 1)
        held_ref[e] = dft(prod, inner_ref, 1)
    merge(held_ref, turn_ref, twid_ref, keep_ref, send_ref)


def backward_kernel(turn_ref, twid_ref, inner_ref, filt_ref, far_ref, sig_ref, *refs):
    slot_refs = slot_list(refs[:10])
    cross_ref, keep_ref, send_ref, held_ref = refs[10:]
    spread(slot_refs, turn_ref, twid_ref, held_ref)
    for e in range(RES):
        freq = dft(held_ref[e], inner_ref, 0)
        re, im = freq[:, :SPAN], freq[:, SPAN:]
        if e < 2:
            sig_re, sig_im = sig_ref[e, :, :SPAN], sig_ref[e, :, SPAN:]
            cross_ref[0, e] = (re * sig_re + im * sig_im) * (1.0 / FULL)
            cross_ref[1, e] = (im * sig_re - re * sig_im) * (1.0 / FULL)
        filt_re, filt_im = filters(filt_ref, far_ref, e)
        prod = jnp.concatenate([filt_re * re + filt_im * im, filt_re * im - filt_im * re], 1)
        held_ref[e] = dft(prod, inner_ref, 1)
    merge(held_ref, turn_ref, twid_ref, keep_ref, send_ref)


PARAMS = pltpu.CompilerParams(vmem_limit_bytes=32 * 1024 * 1024)


def transform_call(kernel, name, kept, consts, filt, far, extra, blocks):
    rows = filt.shape[2]
    operands = (*consts, filt, far, *extra, *blocks)
    return pl.pallas_call(
        kernel,
        out_shape=(
            kept,
            jax.ShapeDtypeStruct((4, rows, SPAN), F32),
            jax.ShapeDtypeStruct((4, rows, SPAN), F32),
        ),
        in_specs=[SMEM] + [VMEM] * (len(operands) - 1),
        out_specs=(VMEM,) * 3,
        scratch_shapes=[pltpu.VMEM((RES, rows, 2 * SPAN), F32)],
        compiler_params=PARAMS,
        cost_estimate=cost(2_000_000_000, 4 << 20),
        name=name,
    )(*operands)


def forward_call(consts, filt, far, blocks):
    kept = jax.ShapeDtypeStruct((2, filt.shape[2], 2 * SPAN), F32)
    return transform_call(forward_kernel, "forward_transform", kept, consts, filt, far, (), blocks)


def backward_call(consts, filt, far, sig_freq, blocks):
    kept = jax.ShapeDtypeStruct(filt.shape, F32)
    return transform_call(
        backward_kernel, "backward_transform", kept, consts, filt, far, (sig_freq,), blocks
    )


def fold_kernel(*refs):
    *in_refs, own_ref, a_ref, b_ref, c_ref = refs
    for k, out in enumerate((own_ref, a_ref, b_ref, c_ref)):
        total = in_refs[0][k].astype(F32)
        for ref in in_refs[1:]:
            total = total + ref[k].astype(F32)
        out[...] = total.astype(out.dtype)


def fold_call(*parts):
    block = parts[0].shape[1:]
    return pl.pallas_call(
        fold_kernel,
        out_shape=(jax.ShapeDtypeStruct(block, F32),) + (jax.ShapeDtypeStruct(block, BF16),) * 3,
        in_specs=[VMEM] * len(parts),
        out_specs=(VMEM,) * 4,
        compiler_params=PARAMS,
        cost_estimate=cost(1 << 20, 2 << 20),
        name="fold",
    )(*parts)


def weight_rows(weight_ref, place_ref, kx, kz, rows):
    start = (place_ref[0] ^ kz) * 4 + (place_ref[1] ^ kx)
    return weight_ref[pl.ds(pl.multiple_of(start * rows, rows), rows), :]


def partial_kernel(place_ref, weight_ref, cot_ref, *out_refs):
    rows = out_refs[0].shape[1]
    for kx in (2, 1, 3, 0):
        for kz in range(4):
            out_refs[kx][kz] = lax.dot_general(
                weight_rows(weight_ref, place_ref, kx, kz, rows),
                cot_ref[...],
                (((1,), (1,)), ((), ())),
                preferred_element_type=F32,
            ).astype(BF16)


def partial_call(place, weight, cot):
    rows = weight.shape[0] // N_CHAN
    return pl.pallas_call(
        partial_kernel,
        out_shape=(jax.ShapeDtypeStruct((4, rows, cot.shape[0]), BF16),) * 4,
        in_specs=[SMEM, VMEM, VMEM],
        out_specs=(VMEM,) * 4,
        compiler_params=PARAMS,
        cost_estimate=cost(268_000_000, 3 << 20),
        name="partial_grad_mixed",
    )(place, weight, cot)


def project_kernel(place_ref, weight_ref, *refs):
    out_ref = refs[-1]
    total = None
    for kx in range(4):
        for kz in range(4):
            block = refs[kx][kz]
            term = lax.dot_general(
                block,
                weight_rows(weight_ref, place_ref, kx, kz, block.shape[0]),
                (((0,), (0,)), ((), ())),
                preferred_element_type=F32,
            )
            total = term if total is None else total + term
    out_ref[...] = total.astype(BF16)


def project_call(place, weight, groups):
    return pl.pallas_call(
        project_kernel,
        out_shape=jax.ShapeDtypeStruct((SPAN, weight.shape[1]), BF16),
        in_specs=[SMEM] + [VMEM] * 5,
        out_specs=VMEM,
        compiler_params=PARAMS,
        cost_estimate=cost(268_000_000, 3 << 20),
        name="project_output",
    )(place, weight, *groups)


def gather_ctx(block):
    far = swap(block, "ctx", 8)
    both = jnp.stack([block, far])
    held = [block, far] + [swap(both, "ctx", 2 * ky) for ky in (1, 2, 3)]
    return held + [swap(part, "ctx", 1) for part in held]


def reduce_ctx(keep, send):
    own, *parts = fold_call(keep, swap(send, "ctx", 1))
    for ky, part in enumerate(parts, 1):
        own = own + swap(part, "ctx", 2 * ky).astype(F32)
    return own


def reduce_chan(parts):
    own, *parts = fold_call(parts[0], *[swap(parts[kx], "chan", kx) for kx in (1, 2, 3)])
    for kz, part in enumerate(parts, 1):
        own = own + swap(part, "chan", 4 * kz).astype(F32)
    return own


def gather_chan(block):
    group = jnp.stack([block] + [swap(block, "chan", 4 * kz) for kz in (1, 2, 3)])
    return [group] + [swap(group, "chan", kx) for kx in (1, 2, 3)]


def body(signal, gating, skip_gain, spectrum, out_weight, cotangent):
    ctx = lax.axis_index("ctx")
    chan = lax.axis_index("chan")
    place = jnp.stack([chan // 4, chan % 4]).astype(jnp.int32)
    turn, twid, inner = tables()
    consts = (
        lax.dynamic_index_in_dim(turn, ctx, 0, keepdims=False),
        lax.dynamic_index_in_dim(twid, ctx, 0, keepdims=False),
        jnp.asarray(inner),
    )
    gate = gating.astype(F32)
    skip = skip_gain[:, None]
    filt = jnp.transpose(spectrum, (0, 2, 1, 3))

    sig_far = swap(signal, "ctx", 8)
    far = swap(filt.astype(BF16), "ctx", 8)
    parts = partial_call(place, out_weight, cotangent)
    got = [swap(parts[kx], "chan", kx) for kx in (1, 2, 3)]
    got[0], got[2], sig_far = fence(got[0], got[2], sig_far)
    folded = fold_call(parts[0], *got)
    both = jnp.stack([signal, sig_far])
    held = [signal, sig_far] + [swap(both, "ctx", 2 * ky) for ky in (1, 2, 3)]
    held, far = fence(held, far)
    sig_blocks = held + [swap(part, "ctx", 1) for part in held]
    grad_mixed, *rest = folded
    for kz, part in enumerate(rest, 1):
        grad_mixed = grad_mixed + swap(part, "chan", 4 * kz).astype(F32)
    grad_pre = (gate * grad_mixed).astype(BF16)
    sig_blocks, grad_pre = fence(sig_blocks, grad_pre)
    grad_far = swap(grad_pre, "ctx", 8)

    sig_freq, conv_keep, conv_send = forward_call(consts, filt, far, sig_blocks)
    conv_keep, conv_send, grad_far = fence(conv_keep, conv_send, grad_far)
    conv = fold_call(conv_keep, swap(conv_send, "ctx", 1))

    conv_own, *rest = conv
    for ky, part in enumerate(rest, 1):
        conv_own = conv_own + swap(part, "ctx", 2 * ky).astype(F32)
    pre_gate = conv_own + skip * signal.astype(F32)
    mixed = (gate * pre_gate).astype(BF16)
    both = jnp.stack([grad_pre, grad_far])
    held = [grad_pre, grad_far] + [swap(both, "ctx", 2 * ky) for ky in (1, 2, 3)]

    group = jnp.stack([mixed] + [swap(mixed, "chan", 4 * kz) for kz in (1, 2, 3)])
    grad_blocks = held + [swap(part, "ctx", 1) for part in held]
    cross, back_keep, back_send = backward_call(consts, filt, far, sig_freq, grad_blocks)
    group, back_keep, back_send = fence(group, back_keep, back_send)
    back = fold_call(back_keep, swap(back_send, "ctx", 1))
    groups = [group] + [swap(group, "chan", kx) for kx in (1, 2, 3)]
    back_own, *rest = back
    for ky, part in enumerate(rest, 1):
        back_own = back_own + swap(part, "ctx", 2 * ky).astype(F32)
    grad_signal = (back_own + skip * grad_pre.astype(F32)).astype(BF16)
    grad_spectrum = jnp.transpose(cross, (0, 2, 1, 3))
    groups, grad_signal, grad_spectrum = fence(groups, grad_signal, grad_spectrum)
    output = project_call(place, out_weight, groups)
    grad_gating = (grad_mixed * pre_gate).astype(BF16)
    return output, grad_signal, grad_gating, grad_spectrum


def solution(mesh):
    placed = (
        P("chan", "ctx"),
        P("chan", "ctx"),
        P("chan"),
        P(None, "chan", "ctx", None),
        P(None, "chan"),
        P("ctx", "chan"),
    )
    return jax.shard_map(
        body,
        mesh=mesh,
        in_specs=placed,
        out_specs=(
            P("ctx", "chan"),
            P("chan", "ctx"),
            P("chan", "ctx"),
            P(None, "chan", "ctx", None),
        ),
        check_vma=False,
    )
```
